32 devices in a mesh: prow: 8 (over z, y), pcol: 4 (over x, core).
Axes of the slice: x: 2, y: 2, z: 4, core: 2. Of those that a mesh axis runs over, the one named last changes fastest.
Arguments:
- panels: float32 [7, 32768], P(None, ('prow', 'pcol')), may hold values from -6 to 8, as said below
- slab_ids: int32 [1024], replicated, may hold values from 0 to 32767, as said below
- pivots: int32 [512], replicated, may hold values from 0 to 65535, as said below
Outputs:
- head: float32 [4, 4, 64, 2, 512], P('pcol')
- lower: float32 [4, 1, 64, 2, 2, 32768], P('pcol', None, None, None, None, 'prow')
- trailing: float32 [4, 3, 64, 2, 2, 32768], P('pcol', None, None, None, None, 'prow')
The draws below stay inside these ranges and needn't reach their ends.
Inputs may be any that keep to these rules, and one draw needn't show every extreme that they name: x in -6 to 6, y in -1 to 1, z in -0.5 to 0 (lid panels have z = 0), area from 0.3 / 256 to 3 / 256, half size 0.02 to 0.05, both self parts 4 to 8. `slab_ids`: 1024 different panel numbers. pivots[2 k] and pivots[2 k + 1] are 2 slab_ids[k] and 2 slab_ids[k] + 1, in either order.
All inputs are finite; a program needn't handle non-finite values.
Results may differ from the reference program's by a relative error of at most 0.0003.
Values sent between devices are 32-bit elements; how exact they have to be, the bound alone decides.
A program may use at most 128 MiB of HBM per device.

```python
import jax
import jax.numpy as jnp
from jax import lax

ROWP = 4096
NC = 1024
KP = 256
NPAN = 32768
CTP = 64
NT = 4
KT = 1
N_PROW = 8
N_PCOL = 4


def slab_order(key):
    middle = (1 + jax.random.permutation(jax.random.fold_in(key, 11), NPAN - 2)).astype(jnp.int32)
    ends = jnp.array([0, NPAN - 1], dtype=jnp.int32)
    first_ids = jnp.concatenate([ends, middle[:KP - 2]])
    first_ids = jax.random.permutation(jax.random.fold_in(key, 12), first_ids)
    return jnp.concatenate([first_ids, middle[KP - 2:NC - 2]]).astype(jnp.int32)


def draw_slab_ids(key, part):
    return slab_order(key)


def draw_pivots(key, part):
    chosen = slab_order(key)[:KP]
    swapped = jax.random.randint(jax.random.fold_in(key, 13), (KP,), 0, 2).astype(jnp.int32)
    first_rows = 2 * chosen + swapped
    second_rows = 2 * chosen + 1 - swapped
    return jnp.stack([first_rows, second_rows], 1).reshape(2 * KP).astype(jnp.int32)


def draw_panels(key, part):
    keys = [jax.random.fold_in(key, 20 + number) for number in range(8)]
    xpos = jax.random.uniform(keys[0], (NPAN,), jnp.float32, -6.0, 6.0)
    ypos = jax.random.uniform(keys[1], (NPAN,), jnp.float32, -1.0, 1.0)
    depth = jax.random.uniform(keys[2], (NPAN,), jnp.float32, 0.0, 0.5)
    lidmask = jax.random.randint(keys[3], (NPAN,), 0, 8) == 0
    zpos = jnp.where(lidmask, 0.0, -depth)
    areas = jnp.exp(jax.random.uniform(keys[4], (NPAN,), jnp.float32, jnp.log(0.3 / KP), jnp.log(3.0 / KP)))
    halfsize = jax.random.uniform(keys[5], (NPAN,), jnp.float32, 0.02, 0.05)
    self_real = jax.random.uniform(keys[6], (NPAN,), jnp.float32, 4.0, 8.0)
    self_imag = jax.random.uniform(keys[7], (NPAN,), jnp.float32, 4.0, 8.0)
    return jnp.stack([xpos, ypos, zpos, areas, halfsize, self_real, self_imag]).astype(jnp.float32)


def setup_inputs(seed: int = 0) -> dict:
    splits = jax.random.split(jax.random.key(seed), 4)
    return {
        "panels": draw_panels(jax.random.fold_in(splits[3], 71), 0),
        "slab_ids": draw_slab_ids(jax.random.fold_in(splits[3], 71), 0),
        "pivots": draw_pivots(jax.random.fold_in(splits[3], 71), 0),
    }


QUAD_OFFSET = 0.5773502691896258
WAVE_NUMBER = 6.0

def influence(row_geometry, row_panels, col_geometry, col_panels):
    target_x = row_geometry[0][None, :]
    target_y = row_geometry[1][None, :]
    target_z = row_geometry[2][None, :]
    source_x = col_geometry[0][:, None]
    source_y = col_geometry[1][:, None]
    source_z = col_geometry[2][:, None]
    areas = col_geometry[3][:, None]
    halfsize = col_geometry[4][:, None]
    halfsq = halfsize * halfsize
    below = target_z - source_z
    mirror = target_z + source_z
    depth_factor = 2.0 * WAVE_NUMBER * jnp.exp(WAVE_NUMBER * mirror)
    real_sum = jnp.zeros(below.shape, row_geometry.dtype)
    imag_sum = jnp.zeros(below.shape, row_geometry.dtype)
    for first_sign in (-1.0, 1.0):
        for second_sign in (-1.0, 1.0):
            delta_x = target_x - (source_x + first_sign * QUAD_OFFSET * halfsize)
            delta_y = target_y - (source_y + second_sign * QUAD_OFFSET * halfsize)
            planar = delta_x * delta_x + delta_y * delta_y + halfsq
            direct = lax.rsqrt(planar + below * below)
            image = lax.rsqrt(planar + mirror * mirror)
            phase = WAVE_NUMBER * jnp.sqrt(planar)
            wave_amp = depth_factor * lax.rsqrt(1.0 + phase)
            real_sum = real_sum + direct + image + wave_amp * jnp.cos(phase)
            imag_sum = imag_sum + wave_amp * jnp.sin(phase)
    same = col_panels[:, None] == row_panels[None, :]
    real_part = 0.25 * areas * real_sum + jnp.where(same, col_geometry[5][:, None], 0.0)
    imag_part = 0.25 * areas * imag_sum + jnp.where(same, col_geometry[6][:, None], 0.0)
    return (real_part, imag_part)

def assemble(real_part, imag_part):
    return jnp.stack([jnp.stack([real_part, imag_part], 1), jnp.stack([-imag_part, real_part], 1)], 1)

def leaf_factor(block):
    count = block.shape[0]
    positions = jnp.arange(count, dtype=jnp.int32)

    def step(column, matrix):
        row_vals = lax.dynamic_index_in_dim(matrix, column, 0, keepdims=False)
        col_vals = lax.dynamic_index_in_dim(matrix, column, 1, keepdims=False)
        pivot_val = lax.dynamic_index_in_dim(row_vals, column, 0, keepdims=False)
        later = positions > column
        factors = jnp.where(later, col_vals / pivot_val, 0.0)
        matrix = matrix - factors[:, None] * jnp.where(later, row_vals, 0.0)[None, :]
        placed = later[:, None] & (positions == column)[None, :]
        return jnp.where(placed, factors[:, None], matrix)
    return lax.fori_loop(0, count, step, block)

def factor(matrix):
    count = matrix.shape[0]
    if count <= 16:
        packed = leaf_factor(matrix)
        return (jnp.tril(packed, -1) + jnp.eye(count, dtype=matrix.dtype), jnp.triu(packed))
    half = count // 2
    lower_one, upper_one = factor(matrix[:half, :half])
    upper_side = jax.scipy.linalg.solve_triangular(lower_one, matrix[:half, half:], lower=True, unit_diagonal=True)
    lower_side = jax.scipy.linalg.solve_triangular(upper_one, matrix[half:, :half].T, trans=1, lower=False).T
    schur = matrix[half:, half:] - jnp.dot(lower_side, upper_side, precision=lax.Precision.HIGHEST)
    lower_two, upper_two = factor(schur)
    zeros_top = jnp.zeros((half, count - half), matrix.dtype)
    lower_all = jnp.concatenate([jnp.concatenate([lower_one, zeros_top], 1), jnp.concatenate([lower_side, lower_two], 1)], 0)
    upper_all = jnp.concatenate([jnp.concatenate([upper_one, upper_side], 1), jnp.concatenate([zeros_top.T, upper_two], 1)], 0)
    return (lower_all, upper_all)

def reference(panels, slab_ids, pivots):
    slab_geometry = panels[:, slab_ids]
    pivot_panels = (pivots // 2).astype(jnp.int32)
    real_part, imag_part = influence(panels[:, pivot_panels], pivot_panels, slab_geometry, slab_ids)
    swapped = (pivots % 2 == 1)[None, :]
    first_col = jnp.where(swapped, imag_part, real_part)
    second_col = jnp.where(swapped, real_part, -imag_part)
    pivot_block = jnp.stack([first_col, second_col], 1).reshape(2 * NC, 2 * KP).T
    lower_factor, upper_factor = factor(pivot_block[:, :2 * KP])
    upper_right = jax.scipy.linalg.solve_triangular(lower_factor, pivot_block[:, 2 * KP:], lower=True, unit_diagonal=True)
    upper_inverse = jax.scipy.linalg.solve_triangular(upper_factor, jnp.eye(2 * KP, dtype=panels.dtype), lower=False)
    coupling = jnp.dot(upper_inverse, upper_right, precision=lax.Precision.HIGHEST)
    packed = jnp.concatenate([jnp.tril(lower_factor, -1) + upper_factor, upper_right], 1)
    head = packed.reshape(2 * KP, NT, N_PCOL, CTP, 2).transpose(2, 1, 3, 4, 0)

    def rows_block(block_index):
        start = (block_index * ROWP).astype(jnp.int32)
        row_geometry = lax.dynamic_slice_in_dim(panels, start, ROWP, 1)
        row_panels = start + jnp.arange(ROWP, dtype=jnp.int32)
        real_rows, imag_rows = influence(row_geometry, row_panels, slab_geometry, slab_ids)
        full = assemble(real_rows, imag_rows).reshape(2 * NC, 2 * ROWP)
        eliminated = full[:2 * KP]
        dims = (((0,), (0,)), ((), ()))
        low = lax.dot_general(upper_inverse, eliminated, dims, precision=lax.Precision.HIGHEST)
        rest = full[2 * KP:] - lax.dot_general(coupling, eliminated, dims, precision=lax.Precision.HIGHEST)
        return (low, rest)
    low, rest = lax.map(rows_block, jnp.arange(N_PROW, dtype=jnp.int32))
    lower = low.reshape(N_PROW, KT, N_PCOL, CTP, 2, 2, ROWP).transpose(2, 1, 3, 4, 5, 0, 6).reshape(N_PCOL, KT, CTP, 2, 2, NPAN)
    trailing = rest.reshape(N_PROW, NT - KT, N_PCOL, CTP, 2, 2, ROWP).transpose(2, 1, 3, 4, 5, 0, 6).reshape(N_PCOL, NT - KT, CTP, 2, 2, NPAN)
    return (head, lower, trailing)
```

```python
import jax
import jax.numpy as jnp
import numpy as np
from jax import lax
from jax.experimental import pallas as pl
from jax.experimental.pallas import tpu as pltpu
from jax.sharding import PartitionSpec as P

QUAD_OFFSET = 0.5773502691896258
WAVE_NUMBER = 6.0
BLOCK = 64


def fit_trig():
    nodes = 0.25 * (1.0 + np.cos(np.pi * (np.arange(400) + 0.5) / 400)) * 0.5
    root = np.sqrt(nodes)
    sine = np.sin(np.pi * root) / root * np.sqrt(2.0)
    cosine = np.cos(np.pi * root) * np.sqrt(2.0)
    powers = nodes[:, None] ** np.arange(5)[None, :]
    return (
        [float(c) for c in np.linalg.lstsq(powers, sine, rcond=None)[0]],
        [float(c) for c in np.linalg.lstsq(powers, cosine, rcond=None)[0]],
    )


SIN_COEF, COS_COEF = fit_trig()


def horner(coef, arg):
    total = coef[-1]
    for value in coef[-2::-1]:
        total = total * arg + value
    return total


def entries(tx, ty, tz, te, tid, left_x, right_x, left_y, right_y, halfsq, sz, se, area, sr, si, sid):
    below = tz - sz
    mirror = tz + sz
    below_sq = below * below
    mirror_sq = mirror * mirror
    squares_x = []
    squares_y = []
    for pos in (left_x, right_x):
        delta = tx - pos
        squares_x.append(delta * delta + halfsq)
    for pos in (left_y, right_y):
        delta = ty - pos
        squares_y.append(delta * delta)
    near = None
    wave_re = None
    wave_im = None
    for sq_x in squares_x:
        for sq_y in squares_y:
            planar = sq_x + sq_y
            both = lax.rsqrt(planar + below_sq) + lax.rsqrt(planar + mirror_sq)
            rho = planar * lax.rsqrt(planar)
            amp = lax.rsqrt(rho * WAVE_NUMBER + 1.0)
            turns = rho * (WAVE_NUMBER / (2.0 * np.pi))
            part = turns - jnp.round(turns)
            part_sq = part * part
            sine = part * horner(SIN_COEF, part_sq)
            cosine = horner(COS_COEF, part_sq)
            scaled = amp * sine
            re = amp - scaled * sine
            im = scaled * cosine
            near = both if near is None else near + both
            wave_re = re if wave_re is None else wave_re + re
            wave_im = im if wave_im is None else wave_im + im
    factor = te * se
    same = tid == sid
    real = area * (near + factor * wave_re) + jnp.where(same, sr, 0.0)
    imag = area * (factor * wave_im) + jnp.where(same, si, 0.0)
    return real, imag


def source_params(geometry, ids):
    offset = QUAD_OFFSET * geometry[4]
    zeros = jnp.zeros_like(offset)
    return jnp.stack(
        [
            geometry[0] - offset,
            geometry[0] + offset,
            geometry[1] - offset,
            geometry[1] + offset,
            geometry[4] * geometry[4],
            geometry[2],
            2.0 * WAVE_NUMBER * jnp.exp(WAVE_NUMBER * geometry[2]),
            0.25 * geometry[3],
            geometry[5],
            geometry[6],
            ids.astype(jnp.float32),
            zeros,
            zeros,
            zeros,
            zeros,
            zeros,
        ]
    )


def target_params(geometry, ids):
    zeros = jnp.zeros_like(geometry[0])
    return jnp.stack(
        [
            geometry[0],
            geometry[1],
            geometry[2],
            jnp.exp(WAVE_NUMBER * geometry[2]),
            ids.astype(jnp.float32),
            zeros,
            zeros,
            zeros,
        ]
    )


def matmul(left, right):
    return jnp.dot(left, right, precision=lax.Precision.HIGHEST, preferred_element_type=jnp.float32)


def cmul(ar, ai, br, bi):
    return matmul(ar, br) - matmul(ai, bi), matmul(ar, bi) + matmul(ai, br)


def invert_block(re, im, rec_r, rec_i):
    size = re.shape[0]
    wide = 2 * size
    rows = lax.broadcasted_iota(jnp.int32, (size, wide), 0)
    lanes = lax.broadcasted_iota(jnp.int32, (size, wide), 1)
    rows_one = lax.broadcasted_iota(jnp.int32, (size, 1), 0)
    eye = jnp.where(
        lax.broadcasted_iota(jnp.int32, (size, size), 0) == lax.broadcasted_iota(jnp.int32, (size, size), 1), 1.0, 0.0
    )
    start_r = jnp.concatenate([re, eye], 1)
    start_i = jnp.concatenate([im, jnp.zeros_like(eye)], 1)

    def step(col, carry):
        mr, mi = carry
        at_lane = lanes == col
        at_row = rows == col
        col_r = jnp.sum(jnp.where(at_lane, mr, 0.0), axis=1, keepdims=True)
        col_i = jnp.sum(jnp.where(at_lane, mi, 0.0), axis=1, keepdims=True)
        row_r = jnp.sum(jnp.where(at_row, mr, 0.0), axis=0, keepdims=True)
        row_i = jnp.sum(jnp.where(at_row, mi, 0.0), axis=0, keepdims=True)
        rec_r[pl.ds(col, 1), :] = row_r
        rec_i[pl.ds(col, 1), :] = row_i
        piv_r = jnp.sum(jnp.where(at_lane[:1], row_r, 0.0), axis=1, keepdims=True)
        piv_i = jnp.sum(jnp.where(at_lane[:1], row_i, 0.0), axis=1, keepdims=True)
        norm = 1.0 / (piv_r * piv_r + piv_i * piv_i)
        inv_r = piv_r * norm
        inv_i = -piv_i * norm
        num_r = jnp.where(rows_one == col, col_r - 1.0, col_r)
        f_r = num_r * inv_r - col_i * inv_i
        f_i = num_r * inv_i + col_i * inv_r
        later = lanes > col
        new_r = mr - (f_r * row_r - f_i * row_i)
        new_i = mi - (f_r * row_i + f_i * row_r)
        out_r = jnp.where(later, new_r, jnp.where(at_lane, f_r, mr))
        out_i = jnp.where(later, new_i, jnp.where(at_lane, f_i, mi))
        return out_r, out_i

    return lax.fori_loop(0, size, step, (start_r, start_i))


def factor_kernel(own_elim, own_trail, tgt, src, own, packed_r, packed_i, head_r, head_i, sol_r, sol_i, rec_r, rec_i, uin_r, uin_i):
    count = tgt.shape[0]
    width = count + own_trail
    for part in range(0, count, 32):
        targets = [tgt[part : part + 32, n : n + 1] for n in range(5)]
        sources = [src[n : n + 1, :] for n in range(11)]
        re, im = entries(*targets, *sources)
        packed_r[part : part + 32, :] = re
        packed_i[part : part + 32, :] = im
    size = BLOCK
    steps = count // size
    rows = lax.broadcasted_iota(jnp.int32, (size, size), 0)
    cols = lax.broadcasted_iota(jnp.int32, (size, size), 1)
    for step in range(steps):
        lo = step * size
        hi = lo + size
        fin_r, fin_i = invert_block(packed_r[lo:hi, lo:hi], packed_i[lo:hi, lo:hi], rec_r, rec_i)
        strict = rows > cols
        low_r = jnp.where(strict, fin_r[:, :size], 0.0)
        low_i = jnp.where(strict, fin_i[:, :size], 0.0)
        eye = jnp.where(rows == cols, 1.0, 0.0)
        uinv_r, uinv_i = cmul(fin_r[:, size:], fin_i[:, size:], low_r + eye, low_i)
        uinv_r = jnp.where(strict, 0.0, uinv_r)
        uinv_i = jnp.where(strict, 0.0, uinv_i)
        uin_r[lo:hi, :] = uinv_r
        uin_i[lo:hi, :] = uinv_i
        linv_r = rec_r[:, size:]
        linv_i = rec_i[:, size:]
        packed_r[lo:hi, lo:hi] = jnp.where(strict, low_r, rec_r[:, :size])
        packed_i[lo:hi, lo:hi] = jnp.where(strict, low_i, rec_i[:, :size])
        up_r, up_i = cmul(linv_r, linv_i, packed_r[lo:hi, hi:width], packed_i[lo:hi, hi:width])
        packed_r[lo:hi, hi:width] = up_r
        packed_i[lo:hi, hi:width] = up_i
        if hi < count:
            dn_r, dn_i = cmul(packed_r[hi:count, lo:hi], packed_i[hi:count, lo:hi], uinv_r, uinv_i)
            packed_r[hi:count, lo:hi] = dn_r
            packed_i[hi:count, lo:hi] = dn_i
            pr, pi = cmul(dn_r, dn_i, up_r, up_i)
            packed_r[hi:count, hi:width] = packed_r[hi:count, hi:width] - pr
            packed_i[hi:count, hi:width] = packed_i[hi:count, hi:width] - pi
    sel_rows = lax.broadcasted_iota(jnp.int32, (count, own_elim), 0)
    select = jnp.where(sel_rows == own[0:1, :], 1.0, 0.0)
    head_r[...] = matmul(packed_r[:, :count], select)
    head_i[...] = matmul(packed_i[:, :count], select)
    for step in range(steps - 1, -1, -1):
        lo = step * size
        hi = lo + size
        rhs_r = jnp.concatenate([select[lo:hi], packed_r[lo:hi, count:width]], 1)
        rhs_i = jnp.concatenate([jnp.zeros_like(select[lo:hi]), packed_i[lo:hi, count:width]], 1)
        if hi < count:
            pr, pi = cmul(
                packed_r[lo:hi, hi:count], packed_i[lo:hi, hi:count], sol_r[hi:count, :], sol_i[hi:count, :]
            )
            rhs_r = rhs_r - pr
            rhs_i = rhs_i - pi
        xr, xi = cmul(uin_r[lo:hi, :], uin_i[lo:hi, :], rhs_r, rhs_i)
        sol_r[lo:hi, :] = xr
        sol_i[lo:hi, :] = xi


def rows_kernel(own_elim, own_trail, count, tgt, src, whi, wlo, fix, lower, trail, ghi, glo, own_r, own_i):
    lanes = tgt.shape[1]
    targets = [tgt[n : n + 1, :] for n in range(5)]

    @pl.loop(0, count // 16)
    def _(group):
        base = pl.multiple_of(group * 16, 16)
        params = src[pl.ds(base, 16), :]
        re, im = entries(*targets, *[params[:, n : n + 1] for n in range(11)])
        for start, value in ((0, re), (count, im)):
            top = value.astype(jnp.bfloat16)
            where = pl.ds(pl.multiple_of(start + base, 16), 16)
            ghi[where, :] = top
            glo[where, :] = (value - top.astype(jnp.float32)).astype(jnp.bfloat16)

    @pl.loop(0, own_trail // 16)
    def _(group):
        base = pl.multiple_of(group * 16, 16)
        params = src[pl.ds(count + base, 16), :]
        re, im = entries(*targets, *[params[:, n : n + 1] for n in range(11)])
        own_r[pl.ds(base, 16), :] = re
        own_i[pl.ds(base, 16), :] = im

    def product(lo, hi):
        total = jnp.dot(whi[lo:hi, :], ghi[...], preferred_element_type=jnp.float32)
        total += jnp.dot(whi[lo:hi, :], glo[...], preferred_element_type=jnp.float32)
        total += jnp.dot(wlo[lo:hi, :], ghi[...], preferred_element_type=jnp.float32)
        return total

    width = own_elim + own_trail
    re = product(0, own_elim)
    im = product(width, width + own_elim)
    for b in range(2):
        fr = fix[:, 2 * b : 2 * b + 1]
        fi = fix[:, 2 * b + 1 : 2 * b + 2]
        lower[:, b, 0, :] = re * fr - im * fi
        lower[:, b, 1, :] = re * fi + im * fr
    re = own_r[...] - product(own_elim, width)
    im = own_i[...] - product(width + own_elim, 2 * width)
    trail[:, 0, 0, :] = re
    trail[:, 0, 1, :] = im
    trail[:, 1, 0, :] = -im
    trail[:, 1, 1, :] = re


def swap_rows(re, im, swapped):
    first = (jnp.where(swapped, im, re), jnp.where(swapped, re, -im))
    second = (jnp.where(swapped, re, im), jnp.where(swapped, -im, re))
    return first, second


def body(panels, slab_ids, pivots):
    col_count = lax.axis_size("pcol")
    pcol_index = lax.axis_index("pcol")
    prow_index = lax.axis_index("prow")
    local_count = panels.shape[1]
    row_geometry = lax.all_gather(panels, "pcol", axis=1, tiled=True)
    row_count = row_geometry.shape[1]
    row_panels = prow_index * row_count + jnp.arange(row_count, dtype=jnp.int32)
    local_panels = (prow_index * col_count + pcol_index) * local_count + jnp.arange(
        local_count, dtype=jnp.int32
    )
    selector = (slab_ids[:, None] == local_panels[None, :]).astype(jnp.float32)
    picked = jnp.dot(panels, selector.T, precision=lax.Precision.HIGHEST)
    slab_geometry = lax.psum(picked, ("prow", "pcol"))
    slab_count = slab_ids.shape[0]
    count = pivots.shape[0] // 2
    tile_width = slab_count // (col_count * col_count)
    panel_tiles = count // (tile_width * col_count)
    own_elim = panel_tiles * tile_width
    own_width = col_count * tile_width
    own_trail = own_width - own_elim
    own_geometry = lax.dynamic_slice_in_dim(
        slab_geometry.reshape(7, col_count, col_count, tile_width), pcol_index, 1, 2
    ).reshape(7, own_width)
    own_panels = lax.dynamic_slice_in_dim(
        slab_ids.reshape(col_count, col_count, tile_width), pcol_index, 1, 1
    ).reshape(own_width)
    src_geometry = jnp.concatenate([slab_geometry[:, :count], own_geometry[:, own_elim:]], 1)
    src_ids = jnp.concatenate([slab_ids[:count], own_panels[own_elim:]])
    src = source_params(src_geometry, src_ids)
    own_index = (
        (jnp.arange(panel_tiles, dtype=jnp.int32)[:, None] * col_count + pcol_index) * tile_width
        + jnp.arange(tile_width, dtype=jnp.int32)[None, :]
    ).reshape(-1)
    own_rows = jnp.broadcast_to(own_index[None, :], (8, own_elim))
    width = count + own_trail
    f32 = jnp.float32
    packed_r, packed_i, head_r, head_i, sol_r, sol_i = pl.pallas_call(
        lambda *refs: factor_kernel(own_elim, own_trail, *refs),
        out_shape=[jax.ShapeDtypeStruct((count, width), f32)] * 2
        + [jax.ShapeDtypeStruct((count, own_elim), f32)] * 2
        + [jax.ShapeDtypeStruct((count, own_width), f32)] * 2,
        scratch_shapes=[pltpu.VMEM((BLOCK, 2 * BLOCK), f32)] * 2 + [pltpu.VMEM((count, BLOCK), f32)] * 2,
        compiler_params=pltpu.CompilerParams(vmem_limit_bytes=32 * 1024 * 1024),
    )(target_params(slab_geometry[:, :count], slab_ids[:count]).T, src, own_rows)

    swapped = pivots[::2] % 2 == 1
    eye = jnp.eye(count, dtype=jnp.bool_)
    diag_r = jnp.sum(jnp.where(eye, packed_r[:, :count], 0.0), axis=1)
    diag_i = jnp.sum(jnp.where(eye, packed_i[:, :count], 0.0), axis=1)
    lam = jnp.where(swapped, diag_r, diag_i) / jnp.where(swapped, diag_i, diag_r)
    own_hot = own_index[:, None] == jnp.arange(count, dtype=jnp.int32)[None, :]
    own_lam = jnp.sum(jnp.where(own_hot, lam[None, :], 0.0), axis=1)
    own_swap = jnp.any(own_hot & swapped[None, :], axis=1)

    full_r = jnp.concatenate([head_r, packed_r[:, count:]], 1).T
    full_i = jnp.concatenate([head_i, packed_i[:, count:]], 1).T
    (a00, a01), (a10, a11) = swap_rows(full_r, full_i, swapped[None, :])
    u00, u01 = a00, a01
    u10 = a10 - lam[None, :] * a00
    u11 = a11 - lam[None, :] * a01
    k_lam = own_lam[:, None]
    k_swap = own_swap[:, None]

    def columns(c0, c1):
        first = jnp.where(k_swap, c1, c0)
        second = jnp.where(k_swap, c0, c1)
        return first + k_lam * second, second

    l00, l01 = columns(a00[:own_elim], a01[:own_elim])
    l10, l11 = columns(a10[:own_elim], a11[:own_elim])
    row_at = jnp.arange(count, dtype=jnp.int32)[None, :]
    is_low = row_at > own_index[:, None]
    is_diag = row_at == own_index[:, None]

    def merge(low, up):
        return jnp.concatenate([jnp.where(is_low, low, up[:own_elim]), up[own_elim:]], 0)

    h00 = merge(l00, u00)
    h01 = merge(l01, u01)
    h10 = merge(l10, u10)
    h10 = jnp.concatenate([jnp.where(is_diag, k_lam, h10[:own_elim]), h10[own_elim:]], 0)
    h11 = merge(l11, u11)
    head = jnp.stack([jnp.stack([h00, h10], 2), jnp.stack([h01, h11], 2)], 1).reshape(
        1, col_count, tile_width, 2, 2 * count
    )

    fix = jnp.stack(
        [
            jnp.where(own_swap, own_lam, 1.0),
            jnp.where(own_swap, 1.0, own_lam),
            jnp.where(own_swap, 1.0, 0.0),
            jnp.where(own_swap, 0.0, 1.0),
        ],
        1,
    )
    wt_r = sol_r.T
    wt_i = sol_i.T
    weights = jnp.concatenate([jnp.concatenate([wt_r, -wt_i], 1), jnp.concatenate([wt_i, wt_r], 1)], 0)
    top = lax.reduce_precision(weights, 8, 7)
    whi = top.astype(jnp.bfloat16)
    wlo = (weights - top).astype(jnp.bfloat16)
    tile = 512
    src_cols = src.T
    lower, trail = pl.pallas_call(
        lambda *refs: rows_kernel(own_elim, own_trail, count, *refs),
        grid=(row_count // tile,),
        in_specs=[
            pl.BlockSpec((8, tile), lambda i: (0, i)),
            pl.BlockSpec(src_cols.shape, lambda i: (0, 0)),
            pl.BlockSpec(whi.shape, lambda i: (0, 0)),
            pl.BlockSpec(wlo.shape, lambda i: (0, 0)),
            pl.BlockSpec(fix.shape, lambda i: (0, 0)),
        ],
        out_specs=[
            pl.BlockSpec((own_elim, 2, 2, tile), lambda i: (0, 0, 0, i)),
            pl.BlockSpec((own_trail, 2, 2, tile), lambda i: (0, 0, 0, i)),
        ],
        out_shape=[
            jax.ShapeDtypeStruct((own_elim, 2, 2, row_count), f32),
            jax.ShapeDtypeStruct((own_trail, 2, 2, row_count), f32),
        ],
        scratch_shapes=[
            pltpu.VMEM((2 * count, tile), jnp.bfloat16),
            pltpu.VMEM((2 * count, tile), jnp.bfloat16),
            pltpu.VMEM((own_trail, tile), f32),
            pltpu.VMEM((own_trail, tile), f32),
        ],
        compiler_params=pltpu.CompilerParams(vmem_limit_bytes=48 * 1024 * 1024),
    )(target_params(row_geometry, row_panels), src_cols, whi, wlo, fix)
    lower_out = lower.reshape(1, panel_tiles, tile_width, 2, 2, row_count)
    trail_out = trail.reshape(1, col_count - panel_tiles, tile_width, 2, 2, row_count)
    return (head, lower_out, trail_out)


def solution(mesh):
    placed = (P(None, ("prow", "pcol")), P(), P())
    return jax.shard_map(
        body,
        mesh=mesh,
        in_specs=placed,
        out_specs=(
            P("pcol", None, None, None, None),
            P("pcol", None, None, None, None, "prow"),
            P("pcol", None, None, None, None, "prow"),
        ),
        check_vma=False,
    )
```

```python
import jax
import jax.numpy as jnp
import numpy as np
from jax import lax
from jax.experimental import pallas as pl
from jax.experimental.pallas import tpu as pltpu
from jax.sharding import PartitionSpec as P

QUAD_OFFSET = 0.5773502691896258
WAVE_NUMBER = 6.0
BLOCK = 64


def fit_trig():
    nodes = 0.25 * (1.0 + np.cos(np.pi * (np.arange(400) + 0.5) / 400)) * 0.5
    root = np.sqrt(nodes)
    sine = np.sin(np.pi * root) / root * np.sqrt(2.0)
    cosine = np.cos(np.pi * root) * np.sqrt(2.0)
    powers = nodes[:, None] ** np.arange(5)[None, :]
    return (
        [float(c) for c in np.linalg.lstsq(powers, sine, rcond=None)[0]],
        [float(c) for c in np.linalg.lstsq(powers, cosine, rcond=None)[0]],
    )


SIN_COEF, COS_COEF = fit_trig()


def horner(coef, arg):
    total = coef[-1]
    for value in coef[-2::-1]:
        total = total * arg + value
    return total


def entries(tx, ty, tz, te, tid, left_x, right_x, left_y, right_y, halfsq, sz, se, area, sr, si, sid):
    below = tz - sz
    mirror = tz + sz
    below_sq = below * below
    mirror_sq = mirror * mirror
    squares_x = []
    squares_y = []
    for pos in (left_x, right_x):
        delta = tx - pos
        squares_x.append(delta * delta + halfsq)
    for pos in (left_y, right_y):
        delta = ty - pos
        squares_y.append(delta * delta)
    near = None
    wave_re = None
    wave_im = None
    for sq_x in squares_x:
        for sq_y in squares_y:
            planar = sq_x + sq_y
            both = lax.rsqrt(planar + below_sq) + lax.rsqrt(planar + mirror_sq)
            rho = planar * lax.rsqrt(planar)
            amp = lax.rsqrt(rho * WAVE_NUMBER + 1.0)
            turns = rho * (WAVE_NUMBER / (2.0 * np.pi))
            part = turns - jnp.round(turns)
            part_sq = part * part
            sine = part * horner(SIN_COEF, part_sq)
            cosine = horner(COS_COEF, part_sq)
            scaled = amp * sine
            re = amp - scaled * sine
            im = scaled * cosine
            near = both if near is None else near + both
            wave_re = re if wave_re is None else wave_re + re
            wave_im = im if wave_im is None else wave_im + im
    factor = te * se
    same = tid == sid
    real = area * (near + factor * wave_re) + jnp.where(same, sr, 0.0)
    imag = area * (factor * wave_im) + jnp.where(same, si, 0.0)
    return real, imag


def source_params(geometry, ids):
    offset = QUAD_OFFSET * geometry[4]
    zeros = jnp.zeros_like(offset)
    return jnp.stack(
        [
            geometry[0] - offset,
            geometry[0] + offset,
            geometry[1] - offset,
            geometry[1] + offset,
            geometry[4] * geometry[4],
            geometry[2],
            2.0 * WAVE_NUMBER * jnp.exp(WAVE_NUMBER * geometry[2]),
            0.25 * geometry[3],
            geometry[5],
            geometry[6],
            ids.astype(jnp.float32),
            zeros,
            zeros,
            zeros,
            zeros,
            zeros,
        ]
    )


def target_params(geometry, ids):
    zeros = jnp.zeros_like(geometry[0])
    return jnp.stack(
        [
            geometry[0],
            geometry[1],
            geometry[2],
            jnp.exp(WAVE_NUMBER * geometry[2]),
            ids.astype(jnp.float32),
            zeros,
            zeros,
            zeros,
        ]
    )


def matmul(left, right):
    return jnp.dot(left, right, precision=lax.Precision.HIGHEST, preferred_element_type=jnp.float32)


def cmul(ar, ai, br, bi):
    return matmul(ar, br) - matmul(ai, bi), matmul(ar, bi) + matmul(ai, br)


def invert_block(re, im, rec_r, rec_i):
    size = re.shape[0]
    wide = 2 * size
    rows = lax.broadcasted_iota(jnp.int32, (size, wide), 0)
    lanes = lax.broadcasted_iota(jnp.int32, (size, wide), 1)
    rows_one = lax.broadcasted_iota(jnp.int32, (size, 1), 0)
    eye = jnp.where(
        lax.broadcasted_iota(jnp.int32, (size, size), 0) == lax.broadcasted_iota(jnp.int32, (size, size), 1), 1.0, 0.0
    )
    start_r = jnp.concatenate([re, eye], 1)
    start_i = jnp.concatenate([im, jnp.zeros_like(eye)], 1)

    def step(col, carry):
        mr, mi = carry
        at_lane = lanes == col
        at_row = rows == col
        col_r = jnp.sum(jnp.where(at_lane, mr, 0.0), axis=1, keepdims=True)
        col_i = jnp.sum(jnp.where(at_lane, mi, 0.0), axis=1, keepdims=True)
        row_r = jnp.sum(jnp.where(at_row, mr, 0.0), axis=0, keepdims=True)
        row_i = jnp.sum(jnp.where(at_row, mi, 0.0), axis=0, keepdims=True)
        rec_r[pl.ds(col, 1), :] = row_r
        rec_i[pl.ds(col, 1), :] = row_i
        piv_r = jnp.sum(jnp.where(at_lane[:1], row_r, 0.0), axis=1, keepdims=True)
        piv_i = jnp.sum(jnp.where(at_lane[:1], row_i, 0.0), axis=1, keepdims=True)
        norm = 1.0 / (piv_r * piv_r + piv_i * piv_i)
        inv_r = piv_r * norm
        inv_i = -piv_i * norm
        num_r = jnp.where(rows_one == col, col_r - 1.0, col_r)
        f_r = num_r * inv_r - col_i * inv_i
        f_i = num_r * inv_i + col_i * inv_r
        later = lanes > col
        new_r = mr - (f_r * row_r - f_i * row_i)
        new_i = mi - (f_r * row_i + f_i * row_r)
        out_r = jnp.where(later, new_r, jnp.where(at_lane, f_r, mr))
        out_i = jnp.where(later, new_i, jnp.where(at_lane, f_i, mi))
        return out_r, out_i

    return lax.fori_loop(0, size, step, (start_r, start_i))


def factor_kernel(own_elim, own_trail, tgt, src, own, packed_r, packed_i, head_r, head_i, sol_r, sol_i, rec_r, rec_i, uin_r, uin_i):
    count = tgt.shape[0]
    width = count + own_trail
    for part in range(0, count, 32):
        targets = [tgt[part : part + 32, n : n + 1] for n in range(5)]
        sources = [src[n : n + 1, :] for n in range(11)]
        re, im = entries(*targets, *sources)
        packed_r[part : part + 32, :] = re
        packed_i[part : part + 32, :] = im
    size = BLOCK
    steps = count // size
    rows = lax.broadcasted_iota(jnp.int32, (size, size), 0)
    cols = lax.broadcasted_iota(jnp.int32, (size, size), 1)
    for step in range(steps):
        lo = step * size
        hi = lo + size
        fin_r, fin_i = invert_block(packed_r[lo:hi, lo:hi], packed_i[lo:hi, lo:hi], rec_r, rec_i)
        strict = rows > cols
        low_r = jnp.where(strict, fin_r[:, :size], 0.0)
        low_i = jnp.where(strict, fin_i[:, :size], 0.0)
        eye = jnp.where(rows == cols, 1.0, 0.0)
        uinv_r, uinv_i = cmul(fin_r[:, size:], fin_i[:, size:], low_r + eye, low_i)
        uinv_r = jnp.where(strict, 0.0, uinv_r)
        uinv_i = jnp.where(strict, 0.0, uinv_i)
        uin_r[lo:hi, :] = uinv_r
        uin_i[lo:hi, :] = uinv_i
        linv_r = rec_r[:, size:]
        linv_i = rec_i[:, size:]
        packed_r[lo:hi, lo:hi] = jnp.where(strict, low_r, rec_r[:, :size])
        packed_i[lo:hi, lo:hi] = jnp.where(strict, low_i, rec_i[:, :size])
        up_r, up_i = cmul(linv_r, linv_i, packed_r[lo:hi, hi:width], packed_i[lo:hi, hi:width])
        packed_r[lo:hi, hi:width] = up_r
        packed_i[lo:hi, hi:width] = up_i
        if hi < count:
            dn_r, dn_i = cmul(packed_r[hi:count, lo:hi], packed_i[hi:count, lo:hi], uinv_r, uinv_i)
            packed_r[hi:count, lo:hi] = dn_r
            packed_i[hi:count, lo:hi] = dn_i
            pr, pi = cmul(dn_r, dn_i, up_r, up_i)
            packed_r[hi:count, hi:width] = packed_r[hi:count, hi:width] - pr
            packed_i[hi:count, hi:width] = packed_i[hi:count, hi:width] - pi
    sel_rows = lax.broadcasted_iota(jnp.int32, (count, own_elim), 0)
    select = jnp.where(sel_rows == own[0:1, :], 1.0, 0.0)
    head_r[...] = matmul(packed_r[:, :count], select)
    head_i[...] = matmul(packed_i[:, :count], select)
    for step in range(steps - 1, -1, -1):
        lo = step * size
        hi = lo + size
        rhs_r = jnp.concatenate([select[lo:hi], packed_r[lo:hi, count:width]], 1)
        rhs_i = jnp.concatenate([jnp.zeros_like(select[lo:hi]), packed_i[lo:hi, count:width]], 1)
        if hi < count:
            pr, pi = cmul(
                packed_r[lo:hi, hi:count], packed_i[lo:hi, hi:count], sol_r[hi:count, :], sol_i[hi:count, :]
            )
            rhs_r = rhs_r - pr
            rhs_i = rhs_i - pi
        xr, xi = cmul(uin_r[lo:hi, :], uin_i[lo:hi, :], rhs_r, rhs_i)
        sol_r[lo:hi, :] = xr
        sol_i[lo:hi, :] = xi


def rows_kernel(own_elim, own_trail, count, tgt, src, whi, wlo, fix, lower, trail, ghi, glo, own_r, own_i):
    lanes = tgt.shape[1]
    def halves(base):
        pieces = []
        for half in range(2):
            params = src[pl.ds(pl.multiple_of(base + 8 * half, 8), 8), :]
            sources = [jnp.broadcast_to(params[:, n : n + 1], (8, 256)) for n in range(11)]
            parts = []
            for lo in range(0, lanes, 256):
                targets = [tgt[n : n + 1, lo : lo + 256] for n in range(5)]
                parts.append(entries(*targets, *sources))
            pieces.append([jnp.concatenate([part[c] for part in parts], 1) for c in range(2)])
        return [jnp.concatenate([piece[c] for piece in pieces], 0) for c in range(2)]

    @pl.loop(0, count // 16)
    def _(group):
        base = pl.multiple_of(group * 16, 16)
        re, im = halves(base)
        for start, value in ((0, re), (count, im)):
            top = value.astype(jnp.bfloat16)
            where = pl.ds(pl.multiple_of(start + base, 16), 16)
            ghi[where, :] = top
            glo[where, :] = (value - top.astype(jnp.float32)).astype(jnp.bfloat16)

    @pl.loop(0, own_trail // 16)
    def _(group):
        base = pl.multiple_of(group * 16, 16)
        re, im = halves(count + base)
        own_r[pl.ds(base, 16), :] = re
        own_i[pl.ds(base, 16), :] = im

    def product(lo, hi):
        total = jnp.dot(whi[lo:hi, :], ghi[...], preferred_element_type=jnp.float32)
        total += jnp.dot(whi[lo:hi, :], glo[...], preferred_element_type=jnp.float32)
        total += jnp.dot(wlo[lo:hi, :], ghi[...], preferred_element_type=jnp.float32)
        return total

    width = own_elim + own_trail
    re = product(0, own_elim)
    im = product(width, width + own_elim)
    for b in range(2):
        fr = fix[:, 2 * b : 2 * b + 1]
        fi = fix[:, 2 * b + 1 : 2 * b + 2]
        lower[:, b, 0, :] = re * fr - im * fi
        lower[:, b, 1, :] = re * fi + im * fr
    re = own_r[...] - product(own_elim, width)
    im = own_i[...] - product(width + own_elim, 2 * width)
    trail[:, 0, 0, :] = re
    trail[:, 0, 1, :] = im
    trail[:, 1, 0, :] = -im
    trail[:, 1, 1, :] = re


def swap_rows(re, im, swapped):
    first = (jnp.where(swapped, im, re), jnp.where(swapped, re, -im))
    second = (jnp.where(swapped, re, im), jnp.where(swapped, -im, re))
    return first, second


def body(panels, slab_ids, pivots):
    col_count = lax.axis_size("pcol")
    pcol_index = lax.axis_index("pcol")
    prow_index = lax.axis_index("prow")
    local_count = panels.shape[1]
    row_geometry = lax.all_gather(panels, "pcol", axis=1, tiled=True)
    row_count = row_geometry.shape[1]
    row_panels = prow_index * row_count + jnp.arange(row_count, dtype=jnp.int32)
    local_panels = (prow_index * col_count + pcol_index) * local_count + jnp.arange(
        local_count, dtype=jnp.int32
    )
    selector = (slab_ids[:, None] == local_panels[None, :]).astype(jnp.float32)
    picked = jnp.dot(panels, selector.T, precision=lax.Precision.HIGHEST)
    slab_geometry = jnp.sum(lax.all_gather(picked, ("prow", "pcol"), axis=0), axis=0)
    slab_count = slab_ids.shape[0]
    count = pivots.shape[0] // 2
    tile_width = slab_count // (col_count * col_count)
    panel_tiles = count // (tile_width * col_count)
    own_elim = panel_tiles * tile_width
    own_width = col_count * tile_width
    own_trail = own_width - own_elim
    own_geometry = lax.dynamic_slice_in_dim(
        slab_geometry.reshape(7, col_count, col_count, tile_width), pcol_index, 1, 2
    ).reshape(7, own_width)
    own_panels = lax.dynamic_slice_in_dim(
        slab_ids.reshape(col_count, col_count, tile_width), pcol_index, 1, 1
    ).reshape(own_width)
    src_geometry = jnp.concatenate([slab_geometry[:, :count], own_geometry[:, own_elim:]], 1)
    src_ids = jnp.concatenate([slab_ids[:count], own_panels[own_elim:]])
    src = source_params(src_geometry, src_ids)
    own_index = (
        (jnp.arange(panel_tiles, dtype=jnp.int32)[:, None] * col_count + pcol_index) * tile_width
        + jnp.arange(tile_width, dtype=jnp.int32)[None, :]
    ).reshape(-1)
    own_rows = jnp.broadcast_to(own_index[None, :], (8, own_elim))
    width = count + own_trail
    f32 = jnp.float32
    packed_r, packed_i, head_r, head_i, sol_r, sol_i = pl.pallas_call(
        lambda *refs: factor_kernel(own_elim, own_trail, *refs),
        out_shape=[jax.ShapeDtypeStruct((count, width), f32)] * 2
        + [jax.ShapeDtypeStruct((count, own_elim), f32)] * 2
        + [jax.ShapeDtypeStruct((count, own_width), f32)] * 2,
        scratch_shapes=[pltpu.VMEM((BLOCK, 2 * BLOCK), f32)] * 2 + [pltpu.VMEM((count, BLOCK), f32)] * 2,
        compiler_params=pltpu.CompilerParams(vmem_limit_bytes=32 * 1024 * 1024),
    )(target_params(slab_geometry[:, :count], slab_ids[:count]).T, src, own_rows)

    swapped = pivots[::2] % 2 == 1
    eye = jnp.eye(count, dtype=jnp.bool_)
    diag_r = jnp.sum(jnp.where(eye, packed_r[:, :count], 0.0), axis=1)
    diag_i = jnp.sum(jnp.where(eye, packed_i[:, :count], 0.0), axis=1)
    lam = jnp.where(swapped, diag_r, diag_i) / jnp.where(swapped, diag_i, diag_r)
    own_hot = own_index[:, None] == jnp.arange(count, dtype=jnp.int32)[None, :]
    own_lam = jnp.sum(jnp.where(own_hot, lam[None, :], 0.0), axis=1)
    own_swap = jnp.any(own_hot & swapped[None, :], axis=1)

    full_r = jnp.concatenate([head_r, packed_r[:, count:]], 1).T
    full_i = jnp.concatenate([head_i, packed_i[:, count:]], 1).T
    (a00, a01), (a10, a11) = swap_rows(full_r, full_i, swapped[None, :])
    u00, u01 = a00, a01
    u10 = a10 - lam[None, :] * a00
    u11 = a11 - lam[None, :] * a01
    k_lam = own_lam[:, None]
    k_swap = own_swap[:, None]

    def columns(c0, c1):
        first = jnp.where(k_swap, c1, c0)
        second = jnp.where(k_swap, c0, c1)
        return first + k_lam * second, second

    l00, l01 = columns(a00[:own_elim], a01[:own_elim])
    l10, l11 = columns(a10[:own_elim], a11[:own_elim])
    row_at = jnp.arange(count, dtype=jnp.int32)[None, :]
    is_low = row_at > own_index[:, None]
    is_diag = row_at == own_index[:, None]

    def merge(low, up):
        return jnp.concatenate([jnp.where(is_low, low, up[:own_elim]), up[own_elim:]], 0)

    h00 = merge(l00, u00)
    h01 = merge(l01, u01)
    h10 = merge(l10, u10)
    h10 = jnp.concatenate([jnp.where(is_diag, k_lam, h10[:own_elim]), h10[own_elim:]], 0)
    h11 = merge(l11, u11)
    head = jnp.stack([jnp.stack([h00, h10], 2), jnp.stack([h01, h11], 2)], 1).reshape(
        1, col_count, tile_width, 2, 2 * count
    )

    fix = jnp.stack(
        [
            jnp.where(own_swap, own_lam, 1.0),
            jnp.where(own_swap, 1.0, own_lam),
            jnp.where(own_swap, 1.0, 0.0),
            jnp.where(own_swap, 0.0, 1.0),
        ],
        1,
    )
    wt_r = sol_r.T
    wt_i = sol_i.T
    weights = jnp.concatenate([jnp.concatenate([wt_r, -wt_i], 1), jnp.concatenate([wt_i, wt_r], 1)], 0)
    top = lax.reduce_precision(weights, 8, 7)
    whi = top.astype(jnp.bfloat16)
    wlo = (weights - top).astype(jnp.bfloat16)
    tile = 512
    src_cols = src.T
    lower, trail = pl.pallas_call(
        lambda *refs: rows_kernel(own_elim, own_trail, count, *refs),
        grid=(row_count // tile,),
        in_specs=[
            pl.BlockSpec((8, tile), lambda i: (0, i)),
            pl.BlockSpec(src_cols.shape, lambda i: (0, 0)),
            pl.BlockSpec(whi.shape, lambda i: (0, 0)),
            pl.BlockSpec(wlo.shape, lambda i: (0, 0)),
            pl.BlockSpec(fix.shape, lambda i: (0, 0)),
        ],
        out_specs=[
            pl.BlockSpec((own_elim, 2, 2, tile), lambda i: (0, 0, 0, i)),
            pl.BlockSpec((own_trail, 2, 2, tile), lambda i: (0, 0, 0, i)),
        ],
        out_shape=[
            jax.ShapeDtypeStruct((own_elim, 2, 2, row_count), f32),
            jax.ShapeDtypeStruct((own_trail, 2, 2, row_count), f32),
        ],
        scratch_shapes=[
            pltpu.VMEM((2 * count, tile), jnp.bfloat16),
            pltpu.VMEM((2 * count, tile), jnp.bfloat16),
            pltpu.VMEM((own_trail, tile), f32),
            pltpu.VMEM((own_trail, tile), f32),
        ],
        compiler_params=pltpu.CompilerParams(vmem_limit_bytes=48 * 1024 * 1024),
    )(target_params(row_geometry, row_panels), src_cols, whi, wlo, fix)
    lower_out = lower.reshape(1, panel_tiles, tile_width, 2, 2, row_count)
    trail_out = trail.reshape(1, col_count - panel_tiles, tile_width, 2, 2, row_count)
    return (head, lower_out, trail_out)


def solution(mesh):
    placed = (P(None, ("prow", "pcol")), P(), P())
    return jax.shard_map(
        body,
        mesh=mesh,
        in_specs=placed,
        out_specs=(
            P("pcol", None, None, None, None),
            P("pcol", None, None, None, None, "prow"),
            P("pcol", None, None, None, None, "prow"),
        ),
        check_vma=False,
    )
```
